32 devices in a mesh: sample: 4 (over y, x), snp: 8 (over z, core).
Axes of the slice: x: 2, y: 2, z: 4, core: 2. Of those that a mesh axis runs over, the one named last changes fastest.
Arguments:
- dosage: bfloat16 [16384, 16384], P('sample', 'snp'), may hold values from 0 to 2, as said below
- allele_mean: float32 [16384], P('snp'), may hold values from 0.1 to 1.9, as said below
- allele_scale: float32 [16384], P('snp'), may hold values from 1.4 to 3.3, as said below
- probes: float32 [192, 16384], P(None, 'sample'), may hold values from -6 to 6
Outputs:
- applied: float32 [192, 16384], P(None, ('sample', 'snp'))
The draws below stay inside these ranges and needn't reach their ends.
Inputs may be any that keep to these rules, and one draw needn't show every extreme that they name: dosage holds only the values 0, 1 and 2. allele_mean is twice an allele frequency between 0.05 and 0.95. allele_scale is 1 / sqrt(allele_mean * (1 - allele_mean / 2)).
All inputs are finite; a program needn't handle non-finite values.
Results may differ from the reference program's by a relative error of at most 0.0058.
Values sent between devices are 32-bit elements; how exact they have to be, the bound alone decides.
No kernel may reach another device: no remote copies, remote signals or barrier semaphores. Data moves between devices by JAX's collectives and lax.ppermute only.
A program may use at most 64 MiB of HBM per device.

```python
import jax
import jax.numpy as jnp
from jax import lax

M = 16384
P_SIZE = 192
ROWS = 4096
N = 16384


def permille(key):
    return jax.random.randint(jax.random.fold_in(key, 7), (M,), 50, 950)


def draw_dosage(key, part):
    freq = permille(key)
    draws = jax.random.randint(jax.random.fold_in(key, 11), (N, M), 0, 1000000)
    first = draws // 1000
    second = draws % 1000
    value = (first < freq[None, :]).astype(jnp.float32) + (second < freq[None, :]).astype(jnp.float32)
    return value.astype(jnp.bfloat16)


def draw_allele_mean(key, part):
    return 2.0 * permille(key).astype(jnp.float32) / 1000.0


def draw_allele_scale(key, part):
    share = permille(key).astype(jnp.float32) / 1000.0
    return 1.0 / jnp.sqrt(2.0 * share * (1.0 - share))


def level_of(key, shape, cuts, low, largest):
    def one(position, blocks):
        heights = jax.random.uniform(jax.random.fold_in(jax.random.fold_in(key, 6), position), (blocks,), jnp.float32, low / len(cuts), largest / len(cuts))
        return jnp.repeat(jnp.exp(heights), shape[position] // blocks).reshape((-1,) + (1,) * (len(shape) - position - 1))

    gain = one(*cuts[0])
    for cut in cuts[1:]:
        gain = gain * one(*cut)
    return gain


def centred(own_key, dims, scale, bound, split=(), held_as=jnp.bfloat16):
    factor_of = level_of(own_key, dims, split, -0.22, 0.18) if split else 1.0
    array = jax.random.normal(own_key, dims, jnp.float32) * scale * factor_of
    return jnp.minimum(jnp.maximum(array, -bound), bound).astype(held_as)


def setup_inputs(seed: int = 0) -> dict:
    keys = jax.random.split(jax.random.key(seed), 5)
    return {
        "dosage": draw_dosage(jax.random.fold_in(keys[4], 71), 0),
        "allele_mean": draw_allele_mean(jax.random.fold_in(keys[4], 71), 0),
        "allele_scale": draw_allele_scale(jax.random.fold_in(keys[4], 71), 0),
        "probes": centred(keys[3], (P_SIZE, N), 1.0, 6.0, ((1, 4),), jnp.float32),
    }


def standard_block(dosage, allele_mean, allele_scale, index):
    block = lax.dynamic_slice_in_dim(dosage, (index * ROWS).astype(jnp.int32), ROWS, 0)
    return ((block.astype(jnp.float32) - allele_mean[None, :]) * allele_scale[None, :]).astype(jnp.bfloat16)

def reference(dosage, allele_mean, allele_scale, probes):
    total = dosage.shape[0]
    width = dosage.shape[1]
    count = total // ROWS
    probe_b = probes.astype(jnp.bfloat16)

    def load_part(index):
        genos = standard_block(dosage, allele_mean, allele_scale, index)
        pslice = lax.dynamic_slice_in_dim(probe_b, (index * ROWS).astype(jnp.int32), ROWS, 1)
        return jnp.dot(pslice, genos, preferred_element_type=jnp.float32)
    loads = lax.optimization_barrier(jnp.sum(lax.map(load_part, jnp.arange(count, dtype=jnp.int32)), axis=0))
    loads_b = (loads / jnp.sqrt(jnp.float32(total))).astype(jnp.bfloat16)

    def apply_part(index):
        genos = standard_block(dosage, allele_mean, allele_scale, index)
        return lax.dot_general(loads_b, genos, (((1,), (1,)), ((), ())), preferred_element_type=jnp.float32)
    parts = lax.map(apply_part, jnp.arange(count, dtype=jnp.int32))
    applied = jnp.transpose(parts, (1, 0, 2)).reshape(loads_b.shape[0], total)
    return applied / jnp.sqrt(jnp.float32(width))
```

```python
import functools

import jax
import jax.numpy as jnp
from jax import lax
from jax.experimental import pallas as pl
from jax.experimental.pallas import tpu as pltpu
from jax.sharding import PartitionSpec as P

AXES = ("sample", "snp")
CHUNKS = (96, 96)
STEPS = 8
LIMIT = 20 * 1024 * 1024
VMEM = pl.BlockSpec(memory_space=pltpu.VMEM)
SMEM = pl.BlockSpec(memory_space=pltpu.SMEM)
HBM = pl.BlockSpec(memory_space=pltpu.HBM)
F32 = jnp.float32
LIGHT = pl.CostEstimate(flops=1, bytes_accessed=1, transcendentals=0)


def pairs(move):
    found = []
    for index in range(32):
        y, x, z, core = index // 16, index // 8 % 2, index // 2 % 4, index % 2
        y, x, z, core = move(y, x, z, core)
        found.append((index, y * 16 + x * 8 + z * 2 + core))
    return found


PLANE_FIRST = pairs(lambda y, x, z, c: (y, 1 - x, z, c) if c == 0 else (1 - y, x, z, c))
PLANE_SECOND = pairs(lambda y, x, z, c: (1 - y, x, z, c) if c == 0 else (y, 1 - x, z, c))
CORES = pairs(lambda y, x, z, c: (y, x, z, 1 - c))
LINE_FIRST = pairs(lambda y, x, z, c: (y, x, z ^ (1 if c == 0 else 2), c))
LINE_SECOND = pairs(lambda y, x, z, c: (y, x, z ^ (2 if c == 0 else 1), c))


def loads_kernel(first, place, probes, dosage, mean, *refs):
    count = len(CHUNKS)
    if first:
        parts, (probe_b, sums, held, wide, middles, sem, sem_p, sem_m) = refs[:count], refs[count:]
    else:
        sums_in, parts, (held, sem) = refs[0], refs[2 : 2 + count], refs[2 + count :]
    slot = 0 if first else 1
    _, rows, width = held.shape
    block = rows // STEPS
    half = 1 - place[0] if first else place[0]
    start = pl.multiple_of(half * width, width)

    def copies(step):
        at = pl.ds(step * block, block)
        made = [pltpu.make_async_copy(dosage.at[at, pl.ds(start, width)], held.at[slot, at], sem.at[step])]
        if first:
            made.append(pltpu.make_async_copy(probes.at[:, at], wide.at[:, at], sem_p.at[step]))
        return made

    for step in range(STEPS):
        for copy in copies(step):
            copy.start()
    if first:
        copy_mean = pltpu.make_async_copy(mean, middles, sem_m)
        copy_mean.start()
    for step in range(STEPS):
        at = pl.ds(step * block, block)
        for copy in copies(step):
            copy.wait()
        if first:
            left = wide[:, at].astype(jnp.bfloat16)
            probe_b[:, at] = left
            share = jnp.sum(left.astype(F32), axis=1, keepdims=True)
            total = share if step == 0 else total + share
        else:
            left = probes[:, at]
        right = held[slot, at]
        low = 0
        for part, many in zip(parts, CHUNKS):
            product = jnp.dot(left[low : low + many], right, preferred_element_type=F32)
            if step == 0:
                part[...] = product
            else:
                part[...] += product
            low += many
    if first:
        sums[...] = jnp.broadcast_to(total, sums.shape)
        copy_mean.wait()
        middle = middles[:, pl.ds(start, width)]
    else:
        total = sums_in[:, :1]
        middle = mean[:, pl.ds(start, width)]
    low = 0
    for part, many in zip(parts, CHUNKS):
        part[...] -= total[low : low + many] * middle
        low += many


def in_hbm(*arrays):
    return [pltpu.with_memory_space_constraint(array, pltpu.HBM) for array in arrays]


def in_vmem(*arrays):
    return [pltpu.with_memory_space_constraint(array, pltpu.VMEM) for array in arrays]


def first_half(place, probes, dosage, mean):
    count, rows = probes.shape
    width = dosage.shape[1] // 2
    return pl.pallas_call(
        functools.partial(loads_kernel, True),
        in_specs=[SMEM, HBM, HBM, HBM],
        out_specs=[VMEM] * (len(CHUNKS) + 3),
        out_shape=[jax.ShapeDtypeStruct((many, width), F32) for many in CHUNKS]
        + [
            jax.ShapeDtypeStruct((count, rows), jnp.bfloat16),
            jax.ShapeDtypeStruct((count, 128), F32),
            pltpu.VMEM((2, rows, width), jnp.bfloat16),
        ],
        scratch_shapes=[
            pltpu.VMEM((count, rows), F32),
            pltpu.VMEM((1, 2 * width), F32),
            pltpu.SemaphoreType.DMA((STEPS,)),
            pltpu.SemaphoreType.DMA((STEPS,)),
            pltpu.SemaphoreType.DMA,
        ],
        compiler_params=pltpu.CompilerParams(vmem_limit_bytes=LIMIT),
        cost_estimate=LIGHT,
        name="loads_sent",
    )(place, *in_hbm(probes, dosage, mean))


def second_half(place, probe_b, dosage, mean, sums, held):
    count, rows = probe_b.shape
    width = dosage.shape[1] // 2
    return pl.pallas_call(
        functools.partial(loads_kernel, False),
        in_specs=[SMEM, VMEM, HBM, VMEM, VMEM, VMEM],
        out_specs=[VMEM] * (len(CHUNKS) + 1),
        out_shape=[jax.ShapeDtypeStruct((many, width), F32) for many in CHUNKS]
        + [pltpu.VMEM((2, rows, width), jnp.bfloat16)],
        scratch_shapes=[pltpu.SemaphoreType.DMA((STEPS,))],
        input_output_aliases={5: len(CHUNKS)},
        compiler_params=pltpu.CompilerParams(vmem_limit_bytes=LIMIT),
        cost_estimate=LIGHT,
        name="loads_kept",
    )(place, probe_b, *in_hbm(dosage), mean, sums, *in_vmem(held))


def apply_kernel(first, factor, shrink, place, *refs):
    if first:
        own, other, mean, scale, held, sent, kept, left_out, shift_out = refs
        half = place[0]
        width = own.shape[1]
        lefts, shift = [], 0.0
        for slot, ref, at in ((0, other, 1 - half), (1, own, half)):
            span = pl.ds(pl.multiple_of(at * width, width), width)
            gain = scale[:, span]
            left = (ref[...] * (gain * gain * factor)).astype(jnp.bfloat16)
            shift = shift + jnp.sum(left.astype(F32) * mean[:, span], axis=1, keepdims=True)
            left_out[slot] = left
            lefts.append(left)
        shift = shift * shrink
        shift_out[...] = jnp.broadcast_to(shift, shift_out.shape)
    else:
        left_in, shift_in, held, sent, kept = refs
        lefts = [left_in[0], left_in[1]]
        shift = shift_in[:, :1]
    core, z = place[1], place[2]
    block = held.shape[1] // 8
    mask = 1 + core
    for out, one, two, owner in ((sent, mask, 3 - mask, 1 - core), (kept, 3 - mask, mask, core)):
        for index, flip in enumerate((two, 3) if first else (0, one)):
            at = pl.ds(pl.multiple_of(((z ^ flip) * 2 + owner) * block, block), block)
            product = 0.0
            for slot, left in enumerate(lefts):
                product = product + lax.dot_general(
                    left, held[slot, at], (((1,), (1,)), ((), ())), preferred_element_type=F32
                )
            out[:, index * block : (index + 1) * block] = product * shrink - shift


def apply_rows(first, factor, shrink, place, *arrays):
    many = arrays[0].shape[-2]
    held = arrays[-1]
    wide = held.shape[1] // 4
    out_shape = [jax.ShapeDtypeStruct((many, wide), F32)] * 2
    if first:
        out_shape += [
            jax.ShapeDtypeStruct((2, many, held.shape[2]), jnp.bfloat16),
            jax.ShapeDtypeStruct((many, 128), F32),
        ]
    return pl.pallas_call(
        functools.partial(apply_kernel, first, factor, shrink),
        in_specs=[SMEM] + [VMEM] * len(arrays),
        out_specs=[VMEM] * len(out_shape),
        out_shape=out_shape,
        compiler_params=pltpu.CompilerParams(vmem_limit_bytes=LIMIT),
        cost_estimate=LIGHT,
        name="apply_first" if first else "apply_second",
    )(place, *arrays[:-1], *in_vmem(held))


def on_slice(dosage, allele_mean, allele_scale, probes):
    total = dosage.shape[0] * lax.axis_size("sample")
    across = dosage.shape[1] * lax.axis_size("snp")
    sample, snp = lax.axis_index("sample"), lax.axis_index("snp")
    core, z = snp % 2, snp // 2
    half = jnp.where(core == 0, sample % 2, sample // 2)
    place = jnp.stack([half, core, z]).astype(jnp.int32)
    mean, scale = allele_mean[None, :], allele_scale[None, :]
    *sent, probe_b, sums, held = first_half(place, probes, dosage, mean)
    *kept, held = second_half(place, probe_b, dosage, mean, sums, held)
    factor, shrink = total**-0.5, across**-0.5
    results = []
    for part, own in zip(sent, kept):
        own = own + lax.ppermute(part, AXES, PLANE_FIRST)
        own = own + lax.ppermute(own, AXES, PLANE_SECOND)
        other = lax.ppermute(own, AXES, PLANE_FIRST)
        sent_a, kept_a, left, shift = apply_rows(True, factor, shrink, place, own, other, mean, scale, held)
        sent_b, kept_b = apply_rows(False, factor, shrink, place, left, shift, held)
        kept_a = kept_a + lax.ppermute(sent_a, AXES, CORES)
        kept_b = kept_b + lax.ppermute(sent_b, AXES, CORES)
        kept_b = kept_b + lax.ppermute(kept_a, AXES, LINE_FIRST)
        width = kept_b.shape[1] // 2
        results.append(kept_b[:, :width] + lax.ppermute(kept_b[:, width:], AXES, LINE_SECOND))
    return jnp.concatenate(results, axis=0)


def on_any(dosage, allele_mean, allele_scale, probes):
    rows = dosage.shape[0]
    total = rows * lax.axis_size("sample")
    width = dosage.shape[1] * lax.axis_size("snp")
    genos = ((dosage.astype(jnp.float32) - allele_mean[None, :]) * allele_scale[None, :]).astype(
        jnp.bfloat16
    )
    probe_b = probes.astype(jnp.bfloat16)
    local = jnp.dot(probe_b, genos, preferred_element_type=jnp.float32)
    loads = lax.psum(local, "sample")
    loads_b = (loads / jnp.sqrt(jnp.float32(total))).astype(jnp.bfloat16)
    partial_rows = lax.dot_general(
        loads_b, genos, (((1,), (1,)), ((), ())), preferred_element_type=jnp.float32
    )
    summed = lax.psum_scatter(partial_rows, "snp", scatter_dimension=1, tiled=True)
    return summed / jnp.sqrt(jnp.float32(width))


def solution(mesh):
    placed = (P("sample", "snp"), P("snp"), P("snp"), P(None, "sample"))
    body = on_slice if (mesh.shape["sample"], mesh.shape["snp"]) == (4, 8) else on_any
    return jax.shard_map(
        body, mesh=mesh, in_specs=placed, out_specs=P(None, ("sample", "snp")), check_vma=False
    )
```

```python
import functools

import jax
import jax.numpy as jnp
from jax import lax
from jax.experimental import pallas as pl
from jax.experimental.pallas import tpu as pltpu
from jax.sharding import PartitionSpec as P

AXES = ("sample", "snp")
CHUNKS = (96, 96)
STEPS = 8
LIMIT = 20 * 1024 * 1024
VMEM = pl.BlockSpec(memory_space=pltpu.VMEM)
SMEM = pl.BlockSpec(memory_space=pltpu.SMEM)
HBM = pl.BlockSpec(memory_space=pltpu.HBM)
ANY = pl.BlockSpec(memory_space=pl.ANY)
F32 = jnp.float32
LIGHT = pl.CostEstimate(flops=1, bytes_accessed=1, transcendentals=0)


def pairs(move):
    found = []
    for index in range(32):
        y, x, z, core = index // 16, index // 8 % 2, index // 2 % 4, index % 2
        y, x, z, core = move(y, x, z, core)
        found.append((index, y * 16 + x * 8 + z * 2 + core))
    return found


PLANE_FIRST = pairs(lambda y, x, z, c: (y, 1 - x, z, c) if c == 0 else (1 - y, x, z, c))
PLANE_SECOND = pairs(lambda y, x, z, c: (1 - y, x, z, c) if c == 0 else (y, 1 - x, z, c))
CORES = pairs(lambda y, x, z, c: (y, x, z, 1 - c))
LINE_FIRST = pairs(lambda y, x, z, c: (y, x, z ^ (1 if c == 0 else 2), c))
LINE_SECOND = pairs(lambda y, x, z, c: (y, x, z ^ (2 if c == 0 else 1), c))


def loads_kernel(first, place, probes, dosage, mean, *refs):
    count = len(CHUNKS)
    if first:
        parts, (probe_b, sums, held, wide, middles, sem, sem_p, sem_m) = refs[:count], refs[count:]
    else:
        sums_in, parts, (held, sem) = refs[0], refs[2 : 2 + count], refs[2 + count :]
    slot = 0 if first else 1
    _, rows, width = held.shape
    block = rows // STEPS
    half = 1 - place[0] if first else place[0]
    start = pl.multiple_of(half * width, width)

    def copies(step):
        at = pl.ds(step * block, block)
        made = [pltpu.make_async_copy(dosage.at[at, pl.ds(start, width)], held.at[slot, at], sem.at[step])]
        if first:
            made.append(pltpu.make_async_copy(probes.at[:, at], wide.at[:, at], sem_p.at[step]))
        return made

    for step in range(STEPS):
        for copy in copies(step):
            copy.start()
    if first:
        copy_mean = pltpu.make_async_copy(mean, middles, sem_m)
        copy_mean.start()
    for step in range(STEPS):
        at = pl.ds(step * block, block)
        for copy in copies(step):
            copy.wait()
        if first:
            left = wide[:, at].astype(jnp.bfloat16)
            probe_b[:, at] = left
            share = jnp.sum(left.astype(F32), axis=1, keepdims=True)
            total = share if step == 0 else total + share
        else:
            left = probes[:, at]
        right = held[slot, at]
        low = 0
        for part, many in zip(parts, CHUNKS):
            product = jnp.dot(left[low : low + many], right, preferred_element_type=F32)
            if step == 0:
                part[...] = product
            else:
                part[...] += product
            low += many
    if first:
        sums[...] = jnp.broadcast_to(total, sums.shape)
        copy_mean.wait()
        middle = middles[:, pl.ds(start, width)]
    else:
        total = sums_in[:, :1]
        middle = mean[:, pl.ds(start, width)]
    low = 0
    for part, many in zip(parts, CHUNKS):
        part[...] -= total[low : low + many] * middle
        low += many


def in_hbm(*arrays):
    return [pltpu.with_memory_space_constraint(array, pltpu.HBM) for array in arrays]


def in_vmem(*arrays):
    return [pltpu.with_memory_space_constraint(array, pltpu.VMEM) for array in arrays]


def first_half(place, probes, dosage, mean):
    count, rows = probes.shape
    width = dosage.shape[1] // 2
    return pl.pallas_call(
        functools.partial(loads_kernel, True),
        in_specs=[SMEM, HBM, HBM, HBM],
        out_specs=[VMEM] * (len(CHUNKS) + 3),
        out_shape=[jax.ShapeDtypeStruct((many, width), F32) for many in CHUNKS]
        + [
            jax.ShapeDtypeStruct((count, rows), jnp.bfloat16),
            jax.ShapeDtypeStruct((count, 128), F32),
            pltpu.VMEM((2, rows, width), jnp.bfloat16),
        ],
        scratch_shapes=[
            pltpu.VMEM((count, rows), F32),
            pltpu.VMEM((1, 2 * width), F32),
            pltpu.SemaphoreType.DMA((STEPS,)),
            pltpu.SemaphoreType.DMA((STEPS,)),
            pltpu.SemaphoreType.DMA,
        ],
        compiler_params=pltpu.CompilerParams(vmem_limit_bytes=LIMIT),
        cost_estimate=LIGHT,
        name="loads_sent",
    )(place, *in_hbm(probes, dosage, mean))


def second_half(place, probe_b, dosage, mean, sums, held):
    count, rows = probe_b.shape
    width = dosage.shape[1] // 2
    return pl.pallas_call(
        functools.partial(loads_kernel, False),
        in_specs=[SMEM, VMEM, HBM] + [VMEM] * 3,
        out_specs=[VMEM] * (len(CHUNKS) + 1),
        out_shape=[jax.ShapeDtypeStruct((many, width), F32) for many in CHUNKS]
        + [pltpu.VMEM((2, rows, width), jnp.bfloat16)],
        scratch_shapes=[pltpu.SemaphoreType.DMA((STEPS,))],
        input_output_aliases={5: len(CHUNKS)},
        compiler_params=pltpu.CompilerParams(vmem_limit_bytes=LIMIT),
        cost_estimate=LIGHT,
        name="loads_kept",
    )(place, probe_b, *in_hbm(dosage), mean, sums, *in_vmem(held))


def add_kernel(count, order, *refs):
    values, outs = refs[:count], refs[count + order :]
    total = values[0][...]
    for value in values[1:]:
        total = total + value[...]
    width = outs[0].shape[1]
    for index, out in enumerate(outs):
        out[...] = total[:, index * width : (index + 1) * width]


def add_up(*arrays, after=(), cut=1):
    many, width = arrays[0].shape
    count = len(arrays)
    return pl.pallas_call(
        functools.partial(add_kernel, count, len(after)),
        in_specs=[VMEM] * count + [ANY] * len(after),
        out_specs=[VMEM] * cut,
        out_shape=[jax.ShapeDtypeStruct((many, width // cut), F32)] * cut,
        compiler_params=pltpu.CompilerParams(vmem_limit_bytes=LIMIT),
        cost_estimate=LIGHT,
        name="add_up",
    )(*arrays, *after)


def apply_kernel(first, swapped, factor, shrink, place, *refs):
    if first:
        own, other, mean, scale, held = refs[:5]
        sent, kept, left_out, shift_out = refs[-4:]
        half = place[0]
        width = own.shape[1]
        lefts, shift = [], 0.0
        for slot, ref, at in ((0, other, 1 - half), (1, own, half)):
            span = pl.ds(pl.multiple_of(at * width, width), width)
            gain = scale[:, span]
            left = (ref[...] * (gain * gain * factor)).astype(jnp.bfloat16)
            shift = shift + jnp.sum(left.astype(F32) * mean[:, span], axis=1, keepdims=True)
            left_out[slot] = left
            lefts.append(left)
        shift = shift * shrink
        shift_out[...] = jnp.broadcast_to(shift, shift_out.shape)
    else:
        left_in, shift_in, held = refs[:3]
        sent, kept = refs[-2:]
        lefts = [left_in[0], left_in[1]]
        shift = shift_in[:, :1]
    core, z = place[1], place[2]
    block = held.shape[1] // 8
    mask = 2 - core if swapped else 1 + core
    for out, one, two, owner in ((sent, mask, 3 - mask, 1 - core), (kept, 3 - mask, mask, core)):
        for index, flip in enumerate((two, 3) if first else (0, one)):
            at = pl.ds(pl.multiple_of(((z ^ flip) * 2 + owner) * block, block), block)
            product = 0.0
            for slot, left in enumerate(lefts):
                product = product + lax.dot_general(
                    left, held[slot, at], (((1,), (1,)), ((), ())), preferred_element_type=F32
                )
            out[:, index * block : (index + 1) * block] = product * shrink - shift


def apply_rows(first, factor, shrink, place, *arrays, after, swapped=False):
    many = arrays[0].shape[-2]
    held = arrays[-1]
    wide = held.shape[1] // 4
    out_shape = [jax.ShapeDtypeStruct((many, wide), F32)] * 2
    if first:
        out_shape += [
            jax.ShapeDtypeStruct((2, many, held.shape[2]), jnp.bfloat16),
            jax.ShapeDtypeStruct((many, 128), F32),
        ]
    return pl.pallas_call(
        functools.partial(apply_kernel, first, swapped, factor, shrink),
        in_specs=[SMEM] + [VMEM] * len(arrays) + [ANY] * len(after),
        out_specs=[VMEM] * len(out_shape),
        out_shape=out_shape,
        compiler_params=pltpu.CompilerParams(vmem_limit_bytes=LIMIT),
        cost_estimate=LIGHT,
        name="apply_first" if first else "apply_second",
    )(place, *arrays[:-1], *in_vmem(held), *after)


def on_slice(dosage, allele_mean, allele_scale, probes):
    total = dosage.shape[0] * lax.axis_size("sample")
    across = dosage.shape[1] * lax.axis_size("snp")
    sample, snp = lax.axis_index("sample"), lax.axis_index("snp")
    core, z = snp % 2, snp // 2
    half = jnp.where(core == 0, sample % 2, sample // 2)
    place = jnp.stack([half, core, z]).astype(jnp.int32)
    mean, scale = allele_mean[None, :], allele_scale[None, :]
    factor, shrink = total**-0.5, across**-0.5
    send = lambda array, moves: lax.ppermute(array, AXES, moves)

    apply_first = functools.partial(apply_rows, True, factor, shrink, place)
    apply_second = functools.partial(apply_rows, False, factor, shrink, place)

    sent_a, sent_b, probe_b, sums, held = first_half(place, probes, dosage, mean)
    got_a, got_b = send(sent_a, PLANE_FIRST), send(sent_b, PLANE_FIRST)
    own_a, own_b, held = second_half(place, probe_b, dosage, mean, sums, held)
    (own_a,) = add_up(own_a, got_a)
    got_a = send(own_a, PLANE_SECOND)
    (own_b,) = add_up(own_b, got_b, after=[own_a])
    got_b = send(own_b, PLANE_SECOND)
    (own_a,) = add_up(own_a, got_a, after=[own_b])
    other_a = send(own_a, PLANE_FIRST)
    (own_b,) = add_up(own_b, got_b, after=[own_a])
    other_b = send(own_b, PLANE_FIRST)
    sent, far_a, left, shift = apply_first(own_a, other_a, mean, scale, held, after=[own_b])
    (far_a,) = add_up(far_a, send(sent, CORES))
    got_a = send(far_a, LINE_FIRST)
    sent, near_a = apply_second(left, shift, held, after=[far_a])
    core_a = send(sent, CORES)
    sent, far_b, left, shift = apply_first(own_b, other_b, mean, scale, held, after=[near_a], swapped=True)
    core_b = send(sent, CORES)
    (near_a,) = add_up(near_a, got_a, after=[far_b])
    near_a, sent_a = add_up(near_a, core_a, cut=2)
    (far_b,) = add_up(far_b, core_b, after=[near_a])
    got_a, got_b = send(sent_a, LINE_SECOND), send(far_b, LINE_SECOND)
    sent, near_b = apply_second(left, shift, held, after=[far_b], swapped=True)
    core_b = send(sent, CORES)
    (near_b,) = add_up(near_b, got_b)
    near_b, sent_b = add_up(near_b, core_b, cut=2)
    got_b = send(sent_b, LINE_FIRST)
    return jnp.concatenate([near_a + got_a, near_b + got_b], axis=0)


def on_any(dosage, allele_mean, allele_scale, probes):
    rows = dosage.shape[0]
    total = rows * lax.axis_size("sample")
    width = dosage.shape[1] * lax.axis_size("snp")
    genos = ((dosage.astype(jnp.float32) - allele_mean[None, :]) * allele_scale[None, :]).astype(
        jnp.bfloat16
    )
    probe_b = probes.astype(jnp.bfloat16)
    local = jnp.dot(probe_b, genos, preferred_element_type=jnp.float32)
    loads = lax.psum(local, "sample")
    loads_b = (loads / jnp.sqrt(jnp.float32(total))).astype(jnp.bfloat16)
    partial_rows = lax.dot_general(
        loads_b, genos, (((1,), (1,)), ((), ())), preferred_element_type=jnp.float32
    )
    summed = lax.psum_scatter(partial_rows, "snp", scatter_dimension=1, tiled=True)
    return summed / jnp.sqrt(jnp.float32(width))


def solution(mesh):
    placed = (P("sample", "snp"), P("snp"), P("snp"), P(None, "sample"))
    body = on_slice if (mesh.shape["sample"], mesh.shape["snp"]) == (4, 8) else on_any
    return jax.shard_map(
        body, mesh=mesh, in_specs=placed, out_specs=P(None, ("sample", "snp")), check_vma=False
    )
```

```python
import functools

import jax
import jax.numpy as jnp
from jax import lax
from jax.experimental import pallas as pl
from jax.experimental.pallas import tpu as pltpu
from jax.sharding import PartitionSpec as P

AXES = ("sample", "snp")
CHUNKS = (96, 96)
STEPS = 8
PIECES = 2
LIMIT = 20 * 1024 * 1024
VMEM = pl.BlockSpec(memory_space=pltpu.VMEM)
SMEM = pl.BlockSpec(memory_space=pltpu.SMEM)
HBM = pl.BlockSpec(memory_space=pltpu.HBM)
ANY = pl.BlockSpec(memory_space=pl.ANY)
F32 = jnp.float32
LIGHT = pl.CostEstimate(flops=1, bytes_accessed=1, transcendentals=0)


def pairs(move):
    found = []
    for index in range(32):
        y, x, z, core = index // 16, index // 8 % 2, index // 2 % 4, index % 2
        y, x, z, core = move(y, x, z, core)
        found.append((index, y * 16 + x * 8 + z * 2 + core))
    return found


PLANE_FIRST = pairs(lambda y, x, z, c: (y, 1 - x, z, c) if c == 0 else (1 - y, x, z, c))
PLANE_SECOND = pairs(lambda y, x, z, c: (1 - y, x, z, c) if c == 0 else (y, 1 - x, z, c))
CORES = pairs(lambda y, x, z, c: (y, x, z, 1 - c))
LINE_FIRST = pairs(lambda y, x, z, c: (y, x, z ^ (1 if c == 0 else 2), c))
LINE_SECOND = pairs(lambda y, x, z, c: (y, x, z ^ (2 if c == 0 else 1), c))


def loads_kernel(first, place, probes, dosage, mean, *refs):
    count = len(CHUNKS)
    if first:
        parts, (probe_b, sums, held, wide, middles, sem, sem_p, sem_m) = refs[:count], refs[count:]
    else:
        sums_in, parts, (held, sem) = refs[0], refs[2 : 2 + count], refs[2 + count :]
    slot = 0 if first else 1
    _, rows, width = held.shape
    block = rows // STEPS
    half = 1 - place[0] if first else place[0]
    start = pl.multiple_of(half * width, width)

    def copies(step):
        at = pl.ds(step * block, block)
        made = [pltpu.make_async_copy(dosage.at[at, pl.ds(start, width)], held.at[slot, at], sem.at[step])]
        if first:
            made.append(pltpu.make_async_copy(probes.at[:, at], wide.at[:, at], sem_p.at[step]))
        return made

    for step in range(STEPS):
        for copy in copies(step):
            copy.start()
    if first:
        copy_mean = pltpu.make_async_copy(mean, middles, sem_m)
        copy_mean.start()
    for step in range(STEPS):
        at = pl.ds(step * block, block)
        for copy in copies(step):
            copy.wait()
        if first:
            left = wide[:, at].astype(jnp.bfloat16)
            probe_b[:, at] = left
            share = jnp.sum(left.astype(F32), axis=1, keepdims=True)
            total = share if step == 0 else total + share
        else:
            left = probes[:, at]
        right = held[slot, at]
        low = 0
        for part, many in zip(parts, CHUNKS):
            product = jnp.dot(left[low : low + many], right, preferred_element_type=F32)
            if step == 0:
                part[...] = product
            else:
                part[...] += product
            low += many
    if first:
        sums[...] = jnp.broadcast_to(total, sums.shape)
        copy_mean.wait()
        middle = middles[:, pl.ds(start, width)]
    else:
        total = sums_in[:, :1]
        middle = mean[:, pl.ds(start, width)]
    low = 0
    for part, many in zip(parts, CHUNKS):
        part[...] -= total[low : low + many] * middle
        low += many


def in_hbm(*arrays):
    return [pltpu.with_memory_space_constraint(array, pltpu.HBM) for array in arrays]


def in_vmem(*arrays):
    return [pltpu.with_memory_space_constraint(array, pltpu.VMEM) for array in arrays]


def first_half(place, probes, dosage, mean):
    count, rows = probes.shape
    width = dosage.shape[1] // 2
    return pl.pallas_call(
        functools.partial(loads_kernel, True),
        in_specs=[SMEM, HBM, HBM, HBM],
        out_specs=[VMEM] * (len(CHUNKS) + 3),
        out_shape=[jax.ShapeDtypeStruct((many, width), F32) for many in CHUNKS]
        + [
            jax.ShapeDtypeStruct((count, rows), jnp.bfloat16),
            jax.ShapeDtypeStruct((count, 128), F32),
            pltpu.VMEM((2, rows, width), jnp.bfloat16),
        ],
        scratch_shapes=[
            pltpu.VMEM((count, rows), F32),
            pltpu.VMEM((1, 2 * width), F32),
            pltpu.SemaphoreType.DMA((STEPS,)),
            pltpu.SemaphoreType.DMA((STEPS,)),
            pltpu.SemaphoreType.DMA,
        ],
        compiler_params=pltpu.CompilerParams(vmem_limit_bytes=LIMIT),
        cost_estimate=LIGHT,
        name="loads_sent",
    )(place, *in_hbm(probes, dosage, mean))


def second_half(place, probe_b, dosage, mean, sums, held):
    count, rows = probe_b.shape
    width = dosage.shape[1] // 2
    return pl.pallas_call(
        functools.partial(loads_kernel, False),
        in_specs=[SMEM, VMEM, HBM] + [VMEM] * 3,
        out_specs=[VMEM] * (len(CHUNKS) + 1),
        out_shape=[jax.ShapeDtypeStruct((many, width), F32) for many in CHUNKS]
        + [pltpu.VMEM((2, rows, width), jnp.bfloat16)],
        scratch_shapes=[pltpu.SemaphoreType.DMA((STEPS,))],
        input_output_aliases={5: len(CHUNKS)},
        compiler_params=pltpu.CompilerParams(vmem_limit_bytes=LIMIT),
        cost_estimate=LIGHT,
        name="loads_kept",
    )(place, probe_b, *in_hbm(dosage), mean, sums, *in_vmem(held))


def add_kernel(count, order, *refs):
    values, outs = refs[:count], refs[count + order :]
    width = outs[0].shape[1]
    whole, pieces = values[0], values[1:]
    if pieces[0].shape[1] < whole.shape[1]:
        narrow = pieces[0].shape[1]
        for index, piece in enumerate(pieces):
            low = index * narrow
            outs[low // width][:, low % width : low % width + narrow] = whole[:, low : low + narrow] + piece[...]
        return
    total = whole[...]
    for value in pieces:
        total = total + value[...]
    for index, out in enumerate(outs):
        out[...] = total[:, index * width : (index + 1) * width]


def add_up(*arrays, after=(), cut=1):
    many, width = arrays[0].shape
    count = len(arrays)
    return pl.pallas_call(
        functools.partial(add_kernel, count, len(after)),
        in_specs=[VMEM] * count + [ANY] * len(after),
        out_specs=[VMEM] * cut,
        out_shape=[jax.ShapeDtypeStruct((many, width // cut), F32)] * cut,
        compiler_params=pltpu.CompilerParams(vmem_limit_bytes=LIMIT),
        cost_estimate=LIGHT,
        name="add_up",
    )(*arrays, *after)


def scaled(ref, gain, middle, factor):
    left = (ref[...] * (gain * gain * factor)).astype(jnp.bfloat16)
    return left, jnp.sum(left.astype(F32) * middle, axis=1, keepdims=True)


def blocks(place, held, swapped):
    core, z = place[1], place[2]
    block = held.shape[1] // 8
    mask = 2 - core if swapped else 1 + core
    flips = [(3 - mask, 1 - core), (3, 1 - core), (mask, core), (3, core)]
    flips += [(0, 1 - core), (mask, 1 - core), (0, core), (3 - mask, core)]
    return [pl.ds(pl.multiple_of(((z ^ flip) * 2 + owner) * block, block), block) for flip, owner in flips]


def times(left, held, slot, at):
    return lax.dot_general(left, held[slot, at], (((1,), (1,)), ((), ())), preferred_element_type=F32)


def half_span(half, width):
    return pl.ds(pl.multiple_of(half * width, width), width)


def own_kernel(swapped, factor, place, own, mean, scale, held, *refs):
    partial, shift_out = refs[-2:]
    span = half_span(place[0], own.shape[1])
    left, shift = scaled(own, scale[:, span], mean[:, span], factor)
    shift_out[...] = jnp.broadcast_to(shift, shift_out.shape)
    block = held.shape[1] // 8
    for index, at in enumerate(blocks(place, held, swapped)):
        partial[:, index * block : (index + 1) * block] = times(left, held, 1, at)


def apply_kernel(first, split, swapped, factor, shrink, place, *refs):
    if first:
        other, own, mean, scale, held = refs[:5]
        *pieces, kept, left_out, shift_out = refs[-3 - PIECES :]
        span = half_span(1 - place[0], other.shape[1])
        left, shift = scaled(other, scale[:, span], mean[:, span], factor)
        left_out[0] = left
        lefts = [left]
        if split:
            partial, shift_own = own, refs[5][:, :1]
        else:
            span = half_span(place[0], own.shape[1])
            left, shift_own = scaled(own, scale[:, span], mean[:, span], factor)
            left_out[1] = left
            lefts.append(left)
        shift = (shift + shift_own) * shrink
        shift_out[...] = jnp.broadcast_to(shift, shift_out.shape)
    else:
        left_in, shift_in, held = refs[:3]
        *pieces, kept = refs[-1 - PIECES :]
        lefts = [left_in[slot] for slot in range(left_in.shape[0])]
        shift = shift_in[:, :1]
        if split:
            partial = refs[3]
    block = held.shape[1] // 8
    skip = 0 if first else 4
    spans = blocks(place, held, swapped)[skip : skip + 4]
    for index, at in enumerate(spans):
        product = 0.0
        if split:
            low = (skip + index) * block
            product = partial[:, low : low + block]
        for slot, left in enumerate(lefts):
            product = product + times(left, held, slot, at)
        product = product * shrink - shift
        outs, start = (pieces, index * block) if index < 2 else ([kept], (index - 2) * block)
        width = outs[0].shape[1]
        step = min(width, block)
        for part in range(0, block, step):
            place_in = start + part
            outs[place_in // width][:, place_in % width : place_in % width + step] = product[:, part : part + step]


def own_rows(factor, place, own, mean, scale, held, after, swapped=False):
    many = own.shape[0]
    return pl.pallas_call(
        functools.partial(own_kernel, swapped, factor),
        in_specs=[SMEM] + [VMEM] * 4 + [ANY] * len(after),
        out_specs=[VMEM] * 2,
        out_shape=[jax.ShapeDtypeStruct((many, held.shape[1]), F32), jax.ShapeDtypeStruct((many, 128), F32)],
        compiler_params=pltpu.CompilerParams(vmem_limit_bytes=LIMIT),
        cost_estimate=LIGHT,
        name="own_rows",
    )(place, own, mean, scale, *in_vmem(held), *after)


def apply_rows(first, factor, shrink, place, *arrays, held, after, split=False, swapped=False):
    many = arrays[0].shape[-2]
    place_of_held = 4 if first else 2
    wide = held.shape[1] // 4
    out_shape = [jax.ShapeDtypeStruct((many, wide // PIECES), F32)] * PIECES
    out_shape += [jax.ShapeDtypeStruct((many, wide), F32)]
    if first:
        out_shape += [
            jax.ShapeDtypeStruct((1 if split else 2, many, held.shape[2]), jnp.bfloat16),
            jax.ShapeDtypeStruct((many, 128), F32),
        ]
    return pl.pallas_call(
        functools.partial(apply_kernel, first, split, swapped, factor, shrink),
        in_specs=[SMEM] + [VMEM] * (len(arrays) + 1) + [ANY] * len(after),
        out_specs=[VMEM] * len(out_shape),
        out_shape=out_shape,
        compiler_params=pltpu.CompilerParams(vmem_limit_bytes=LIMIT),
        cost_estimate=LIGHT,
        name="apply_first" if first else "apply_second",
    )(place, *arrays[:place_of_held], *in_vmem(held), *arrays[place_of_held:], *after)


def on_slice(dosage, allele_mean, allele_scale, probes):
    total = dosage.shape[0] * lax.axis_size("sample")
    across = dosage.shape[1] * lax.axis_size("snp")
    sample, snp = lax.axis_index("sample"), lax.axis_index("snp")
    core, z = snp % 2, snp // 2
    half = jnp.where(core == 0, sample % 2, sample // 2)
    place = jnp.stack([half, core, z]).astype(jnp.int32)
    mean, scale = allele_mean[None, :], allele_scale[None, :]
    factor, shrink = total**-0.5, across**-0.5
    send = lambda array, moves: lax.ppermute(array, AXES, moves)

    apply_first = functools.partial(apply_rows, True, factor, shrink, place)
    apply_second = functools.partial(apply_rows, False, factor, shrink, place)

    sent_a, sent_b, probe_b, sums, held = first_half(place, probes, dosage, mean)
    got_a, got_b = send(sent_a, PLANE_FIRST), send(sent_b, PLANE_FIRST)
    own_a, own_b, held = second_half(place, probe_b, dosage, mean, sums, held)
    (own_a,) = add_up(own_a, got_a)
    got_a = send(own_a, PLANE_SECOND)
    (own_b,) = add_up(own_b, got_b, after=[own_a])
    got_b = send(own_b, PLANE_SECOND)
    (own_a,) = add_up(own_a, got_a, after=[own_b])
    other_a = send(own_a, PLANE_FIRST)
    part_a, shift_a = own_rows(factor, place, own_a, mean, scale, held, after=[])
    (own_b,) = add_up(own_b, got_b, after=[part_a])
    other_b = send(own_b, PLANE_FIRST)
    *sent, far_a, left_a, shift_a = apply_first(
        other_a, part_a, mean, scale, shift_a, held=held, after=[own_b], split=True
    )
    (far_a,) = add_up(far_a, *[send(piece, CORES) for piece in sent])
    got_a = send(far_a, LINE_FIRST)
    *sent, near_a = apply_second(left_a, shift_a, part_a, held=held, after=[far_a], split=True)
    core_a = [send(piece, CORES) for piece in sent]
    *sent, far_b, left_b, shift_b = apply_first(
        other_b, own_b, mean, scale, held=held, after=[near_a], swapped=True
    )
    (far_b,) = add_up(far_b, *[send(piece, CORES) for piece in sent])
    got_b = send(far_b, LINE_SECOND)
    (near_a,) = add_up(near_a, got_a, after=[far_b])
    near_a, sent_a = add_up(near_a, *core_a, cut=2)
    got_a = send(sent_a, LINE_SECOND)
    *sent, near_b = apply_second(left_b, shift_b, held=held, after=[near_a], swapped=True)
    core_b = [send(piece, CORES) for piece in sent]
    (near_b,) = add_up(near_b, got_b, after=[near_a])
    near_b, sent_b = add_up(near_b, *core_b, cut=2)
    got_b = send(sent_b, LINE_FIRST)
    return jnp.concatenate([near_a + got_a, near_b + got_b], axis=0)


def on_any(dosage, allele_mean, allele_scale, probes):
    rows = dosage.shape[0]
    total = rows * lax.axis_size("sample")
    width = dosage.shape[1] * lax.axis_size("snp")
    genos = ((dosage.astype(jnp.float32) - allele_mean[None, :]) * allele_scale[None, :]).astype(
        jnp.bfloat16
    )
    probe_b = probes.astype(jnp.bfloat16)
    local = jnp.dot(probe_b, genos, preferred_element_type=jnp.float32)
    loads = lax.psum(local, "sample")
    loads_b = (loads / jnp.sqrt(jnp.float32(total))).astype(jnp.bfloat16)
    partial_rows = lax.dot_general(
        loads_b, genos, (((1,), (1,)), ((), ())), preferred_element_type=jnp.float32
    )
    summed = lax.psum_scatter(partial_rows, "snp", scatter_dimension=1, tiled=True)
    return summed / jnp.sqrt(jnp.float32(width))


def solution(mesh):
    placed = (P("sample", "snp"), P("snp"), P("snp"), P(None, "sample"))
    body = on_slice if (mesh.shape["sample"], mesh.shape["snp"]) == (4, 8) else on_any
    return jax.shard_map(
        body, mesh=mesh, in_specs=placed, out_specs=P(None, ("sample", "snp")), check_vma=False
    )
```

```python
import functools

import jax
import jax.numpy as jnp
from jax import lax
from jax.experimental import pallas as pl
from jax.experimental.pallas import tpu as pltpu
from jax.sharding import PartitionSpec as P

AXES = ("sample", "snp")
CHUNKS = (112, 80)
STEPS = 8
PIECES = 2
LIMIT = 20 * 1024 * 1024
VMEM = pl.BlockSpec(memory_space=pltpu.VMEM)
SMEM = pl.BlockSpec(memory_space=pltpu.SMEM)
HBM = pl.BlockSpec(memory_space=pltpu.HBM)
ANY = pl.BlockSpec(memory_space=pl.ANY)
F32 = jnp.float32
LIGHT = pl.CostEstimate(flops=1, bytes_accessed=1, transcendentals=0)


def pairs(move):
    found = []
    for index in range(32):
        y, x, z, core = index // 16, index // 8 % 2, index // 2 % 4, index % 2
        y, x, z, core = move(y, x, z, core)
        found.append((index, y * 16 + x * 8 + z * 2 + core))
    return found


PLANE_FIRST = pairs(lambda y, x, z, c: (y, 1 - x, z, c) if c == 0 else (1 - y, x, z, c))
PLANE_SECOND = pairs(lambda y, x, z, c: (1 - y, x, z, c) if c == 0 else (y, 1 - x, z, c))
CORES = pairs(lambda y, x, z, c: (y, x, z, 1 - c))
LINE_FIRST = pairs(lambda y, x, z, c: (y, x, z ^ (1 if c == 0 else 2), c))
LINE_SECOND = pairs(lambda y, x, z, c: (y, x, z ^ (2 if c == 0 else 1), c))


def loads_kernel(first, place, probes, dosage, mean, *refs):
    count = len(CHUNKS)
    if first:
        parts, (probe_b, sums, held, wide, middles, sem, sem_p, sem_m) = refs[:count], refs[count:]
    else:
        sums_in, parts, (held, sem) = refs[0], refs[2 : 2 + count], refs[2 + count :]
    slot = 0 if first else 1
    _, rows, width = held.shape
    block = rows // STEPS
    half = 1 - place[0] if first else place[0]
    start = pl.multiple_of(half * width, width)

    def copies(step):
        at = pl.ds(step * block, block)
        made = [pltpu.make_async_copy(dosage.at[at, pl.ds(start, width)], held.at[slot, at], sem.at[step])]
        if first:
            made.append(pltpu.make_async_copy(probes.at[:, at], wide.at[:, at], sem_p.at[step]))
        return made

    for step in range(STEPS):
        for copy in copies(step):
            copy.start()
    if first:
        copy_mean = pltpu.make_async_copy(mean, middles, sem_m)
        copy_mean.start()
    for step in range(STEPS):
        at = pl.ds(step * block, block)
        for copy in copies(step):
            copy.wait()
        if first:
            left = wide[:, at].astype(jnp.bfloat16)
            probe_b[:, at] = left
            share = jnp.sum(left.astype(F32), axis=1, keepdims=True)
            total = share if step == 0 else total + share
        else:
            left = probes[:, at]
        right = held[slot, at]
        low = 0
        for part, many in zip(parts, CHUNKS):
            product = jnp.dot(left[low : low + many], right, preferred_element_type=F32)
            if step == 0:
                part[...] = product
            else:
                part[...] += product
            low += many
    if first:
        sums[...] = jnp.broadcast_to(total, sums.shape)
        copy_mean.wait()
        middle = middles[:, pl.ds(start, width)]
    else:
        total = sums_in[:, :1]
        middle = mean[:, pl.ds(start, width)]
    low = 0
    for part, many in zip(parts, CHUNKS):
        part[...] -= total[low : low + many] * middle
        low += many


def in_hbm(*arrays):
    return [pltpu.with_memory_space_constraint(array, pltpu.HBM) for array in arrays]


def in_vmem(*arrays):
    return [pltpu.with_memory_space_constraint(array, pltpu.VMEM) for array in arrays]


def first_half(place, probes, dosage, mean):
    count, rows = probes.shape
    width = dosage.shape[1] // 2
    return pl.pallas_call(
        functools.partial(loads_kernel, True),
        in_specs=[SMEM, HBM, HBM, HBM],
        out_specs=[VMEM] * (len(CHUNKS) + 3),
        out_shape=[jax.ShapeDtypeStruct((many, width), F32) for many in CHUNKS]
        + [
            jax.ShapeDtypeStruct((count, rows), jnp.bfloat16),
            jax.ShapeDtypeStruct((count, 128), F32),
            pltpu.VMEM((2, rows, width), jnp.bfloat16),
        ],
        scratch_shapes=[
            pltpu.VMEM((count, rows), F32),
            pltpu.VMEM((1, 2 * width), F32),
            pltpu.SemaphoreType.DMA((STEPS,)),
            pltpu.SemaphoreType.DMA((STEPS,)),
            pltpu.SemaphoreType.DMA,
        ],
        compiler_params=pltpu.CompilerParams(vmem_limit_bytes=LIMIT),
        cost_estimate=LIGHT,
        name="loads_sent",
    )(place, *in_hbm(probes, dosage, mean))


def second_half(place, probe_b, dosage, mean, sums, held):
    count, rows = probe_b.shape
    width = dosage.shape[1] // 2
    return pl.pallas_call(
        functools.partial(loads_kernel, False),
        in_specs=[SMEM, VMEM, HBM] + [VMEM] * 3,
        out_specs=[VMEM] * (len(CHUNKS) + 1),
        out_shape=[jax.ShapeDtypeStruct((many, width), F32) for many in CHUNKS]
        + [pltpu.VMEM((2, rows, width), jnp.bfloat16)],
        scratch_shapes=[pltpu.SemaphoreType.DMA((STEPS,))],
        input_output_aliases={5: len(CHUNKS)},
        compiler_params=pltpu.CompilerParams(vmem_limit_bytes=LIMIT),
        cost_estimate=LIGHT,
        name="loads_kept",
    )(place, probe_b, *in_hbm(dosage), mean, sums, *in_vmem(held))


def add_kernel(count, order, *refs):
    values, outs = refs[:count], refs[count + order :]
    width = outs[0].shape[1]
    whole, pieces = values[0], values[1:]
    if pieces[0].shape[1] < whole.shape[1]:
        narrow = pieces[0].shape[1]
        for index, piece in enumerate(pieces):
            low = index * narrow
            outs[low // width][:, low % width : low % width + narrow] = whole[:, low : low + narrow] + piece[...]
        return
    total = whole[...]
    for value in pieces:
        total = total + value[...]
    for index, out in enumerate(outs):
        out[...] = total[:, index * width : (index + 1) * width]


def add_up(*arrays, after=(), cut=1):
    many, width = arrays[0].shape
    count = len(arrays)
    return pl.pallas_call(
        functools.partial(add_kernel, count, len(after)),
        in_specs=[VMEM] * count + [ANY] * len(after),
        out_specs=[VMEM] * cut,
        out_shape=[jax.ShapeDtypeStruct((many, width // cut), F32)] * cut,
        compiler_params=pltpu.CompilerParams(vmem_limit_bytes=LIMIT),
        cost_estimate=LIGHT,
        name="add_up",
    )(*arrays, *after)


def halves_kernel(count, *refs):
    whole, received, (out, *halves) = refs[0], refs[1 : 1 + count], refs[-3:]
    width = halves[0].shape[1]
    for index, half in enumerate(halves):
        at = slice(index * width, (index + 1) * width)
        value = whole[:, at] + (received[0][:, at] if count == 1 else received[index][...])
        out[:, at] = value
        half[...] = value


def add_halves(whole, received, after=()):
    many, width = whole.shape
    return pl.pallas_call(
        functools.partial(halves_kernel, len(received)),
        in_specs=[VMEM] * (1 + len(received)) + [ANY] * len(after),
        out_specs=[VMEM] * 3,
        out_shape=[jax.ShapeDtypeStruct((many, wide), F32) for wide in (width, width // 2, width // 2)],
        compiler_params=pltpu.CompilerParams(vmem_limit_bytes=LIMIT),
        cost_estimate=LIGHT,
        name="add_halves",
    )(whole, *received, *after)


def scaled(loads, gain, middle, factor):
    left = (loads * (gain * gain * factor)).astype(jnp.bfloat16)
    return left, jnp.sum(left.astype(F32) * middle, axis=1, keepdims=True)


def blocks(place, held, swapped):
    core, z = place[1], place[2]
    block = held.shape[1] // 8
    mask = 2 - core if swapped else 1 + core
    flips = [(3 - mask, 1 - core), (3, 1 - core), (mask, core), (3, core)]
    flips += [(0, 1 - core), (mask, 1 - core), (0, core), (3 - mask, core)]
    return [pl.ds(pl.multiple_of(((z ^ flip) * 2 + owner) * block, block), block) for flip, owner in flips]


def times(left, held, slot, at):
    return lax.dot_general(left, held[slot, at], (((1,), (1,)), ((), ())), preferred_element_type=F32)


def half_span(half, width):
    return pl.ds(pl.multiple_of(half * width, width), width)


def own_kernel(swapped, factor, place, own, mean, scale, held, *refs):
    partial, shift_out = refs[-2:]
    span = half_span(place[0], own.shape[1])
    left, shift = scaled(own[...], scale[:, span], mean[:, span], factor)
    shift_out[...] = jnp.broadcast_to(shift, shift_out.shape)
    block = held.shape[1] // 8
    for index, at in enumerate(blocks(place, held, swapped)):
        partial[:, index * block : (index + 1) * block] = times(left, held, 1, at)


def apply_kernel(first, split, swapped, factor, shrink, place, *refs):
    if first:
        other, own, mean, scale, held = refs[:5]
        *pieces, kept, left_out, shift_out = refs[-3 - PIECES :]
        other = other[...]
        if split:
            other = jnp.concatenate([other, refs[6][...]], axis=1)
        span = half_span(1 - place[0], other.shape[1])
        left, shift = scaled(other, scale[:, span], mean[:, span], factor)
        left_out[0] = left
        lefts = [left]
        if split:
            partial, shift_own = own, refs[5][:, :1]
        else:
            span = half_span(place[0], own.shape[1])
            left, shift_own = scaled(own[...], scale[:, span], mean[:, span], factor)
            left_out[1] = left
            lefts.append(left)
        shift = (shift + shift_own) * shrink
        shift_out[...] = jnp.broadcast_to(shift, shift_out.shape)
    else:
        left_in, shift_in, held = refs[:3]
        *pieces, kept = refs[-1 - PIECES :]
        lefts = [left_in[slot] for slot in range(left_in.shape[0])]
        shift = shift_in[:, :1]
        if split:
            partial = refs[3]
    block = held.shape[1] // 8
    skip = 0 if first else 4
    spans = blocks(place, held, swapped)[skip : skip + 4]
    for index, at in enumerate(spans):
        product = 0.0
        if split:
            low = (skip + index) * block
            product = partial[:, low : low + block]
        for slot, left in enumerate(lefts):
            product = product + times(left, held, slot, at)
        product = product * shrink - shift
        outs, start = (pieces, index * block) if index < 2 else ([kept], (index - 2) * block)
        width = outs[0].shape[1]
        step = min(width, block)
        for part in range(0, block, step):
            place_in = start + part
            outs[place_in // width][:, place_in % width : place_in % width + step] = product[:, part : part + step]


def own_rows(factor, place, own, mean, scale, held, after, swapped=False):
    many = own.shape[0]
    return pl.pallas_call(
        functools.partial(own_kernel, swapped, factor),
        in_specs=[SMEM] + [VMEM] * 4 + [ANY] * len(after),
        out_specs=[VMEM] * 2,
        out_shape=[jax.ShapeDtypeStruct((many, held.shape[1]), F32), jax.ShapeDtypeStruct((many, 128), F32)],
        compiler_params=pltpu.CompilerParams(vmem_limit_bytes=LIMIT),
        cost_estimate=LIGHT,
        name="own_rows",
    )(place, own, mean, scale, *in_vmem(held), *after)


def apply_rows(first, factor, shrink, place, *arrays, held, after, split=False, swapped=False):
    many = arrays[0].shape[-2]
    place_of_held = 4 if first else 2
    wide = held.shape[1] // 4
    out_shape = [jax.ShapeDtypeStruct((many, wide // PIECES), F32)] * PIECES
    out_shape += [jax.ShapeDtypeStruct((many, wide), F32)]
    if first:
        out_shape += [
            jax.ShapeDtypeStruct((1 if split else 2, many, held.shape[2]), jnp.bfloat16),
            jax.ShapeDtypeStruct((many, 128), F32),
        ]
    return pl.pallas_call(
        functools.partial(apply_kernel, first, split, swapped, factor, shrink),
        in_specs=[SMEM] + [VMEM] * (len(arrays) + 1) + [ANY] * len(after),
        out_specs=[VMEM] * len(out_shape),
        out_shape=out_shape,
        compiler_params=pltpu.CompilerParams(vmem_limit_bytes=LIMIT),
        cost_estimate=LIGHT,
        name="apply_first" if first else "apply_second",
    )(place, *arrays[:place_of_held], *in_vmem(held), *arrays[place_of_held:], *after)


def on_slice(dosage, allele_mean, allele_scale, probes):
    total = dosage.shape[0] * lax.axis_size("sample")
    across = dosage.shape[1] * lax.axis_size("snp")
    sample, snp = lax.axis_index("sample"), lax.axis_index("snp")
    core, z = snp % 2, snp // 2
    half = jnp.where(core == 0, sample % 2, sample // 2)
    place = jnp.stack([half, core, z]).astype(jnp.int32)
    mean, scale = allele_mean[None, :], allele_scale[None, :]
    factor, shrink = total**-0.5, across**-0.5
    send = lambda array, moves: lax.ppermute(array, AXES, moves)

    apply_first = functools.partial(apply_rows, True, factor, shrink, place)
    apply_second = functools.partial(apply_rows, False, factor, shrink, place)

    sent_a, sent_b, probe_b, sums, held = first_half(place, probes, dosage, mean)
    got_a, got_b = send(sent_a, PLANE_FIRST), send(sent_b, PLANE_FIRST)
    own_a, own_b, held = second_half(place, probe_b, dosage, mean, sums, held)
    own_a, *parts = add_halves(own_a, [got_a])
    got_a = [send(part, PLANE_SECOND) for part in parts]
    (own_b,) = add_up(own_b, got_b, after=[own_a])
    got_b = send(own_b, PLANE_SECOND)
    own_a, *parts = add_halves(own_a, got_a, after=[own_b])
    other_a = [send(part, PLANE_FIRST) for part in parts]
    part_a, shift_a = own_rows(factor, place, own_a, mean, scale, held, after=[])
    (own_b,) = add_up(own_b, got_b, after=[part_a])
    other_b = send(own_b, PLANE_FIRST)
    *sent, far_a, left_a, shift_a = apply_first(
        other_a[0], part_a, mean, scale, shift_a, other_a[1], held=held, after=[own_b], split=True
    )
    (far_a,) = add_up(far_a, *[send(piece, CORES) for piece in sent])
    got_a = send(far_a, LINE_FIRST)
    *sent, near_a = apply_second(left_a, shift_a, part_a, held=held, after=[far_a], split=True)
    core_a = [send(piece, CORES) for piece in sent]
    *sent, far_b, left_b, shift_b = apply_first(
        other_b, own_b, mean, scale, held=held, after=[near_a], swapped=True
    )
    (far_b,) = add_up(far_b, *[send(piece, CORES) for piece in sent])
    got_b = send(far_b, LINE_SECOND)
    (near_a,) = add_up(near_a, got_a, after=[far_b])
    near_a, sent_a = add_up(near_a, *core_a, cut=2)
    got_a = send(sent_a, LINE_SECOND)
    *sent, near_b = apply_second(left_b, shift_b, held=held, after=[near_a], swapped=True)
    core_b = [send(piece, CORES) for piece in sent]
    (near_b,) = add_up(near_b, got_b, after=[near_a])
    near_b, sent_b = add_up(near_b, *core_b, cut=2)
    got_b = send(sent_b, LINE_FIRST)
    return jnp.concatenate([near_a + got_a, near_b + got_b], axis=0)


def on_any(dosage, allele_mean, allele_scale, probes):
    rows = dosage.shape[0]
    total = rows * lax.axis_size("sample")
    width = dosage.shape[1] * lax.axis_size("snp")
    genos = ((dosage.astype(jnp.float32) - allele_mean[None, :]) * allele_scale[None, :]).astype(
        jnp.bfloat16
    )
    probe_b = probes.astype(jnp.bfloat16)
    local = jnp.dot(probe_b, genos, preferred_element_type=jnp.float32)
    loads = lax.psum(local, "sample")
    loads_b = (loads / jnp.sqrt(jnp.float32(total))).astype(jnp.bfloat16)
    partial_rows = lax.dot_general(
        loads_b, genos, (((1,), (1,)), ((), ())), preferred_element_type=jnp.float32
    )
    summed = lax.psum_scatter(partial_rows, "snp", scatter_dimension=1, tiled=True)
    return summed / jnp.sqrt(jnp.float32(width))


def solution(mesh):
    placed = (P("sample", "snp"), P("snp"), P("snp"), P(None, "sample"))
    body = on_slice if (mesh.shape["sample"], mesh.shape["snp"]) == (4, 8) else on_any
    return jax.shard_map(
        body, mesh=mesh, in_specs=placed, out_specs=P(None, ("sample", "snp")), check_vma=False
    )
```

```python
import functools

import jax
import jax.numpy as jnp
from jax import lax
from jax.experimental import pallas as pl
from jax.experimental.pallas import tpu as pltpu
from jax.sharding import PartitionSpec as P

AXES = ("sample", "snp")
CHUNKS = (112, 80)
STEPS = 8
PIECES = 2
LIMIT = 20 * 1024 * 1024
VMEM = pl.BlockSpec(memory_space=pltpu.VMEM)
SMEM = pl.BlockSpec(memory_space=pltpu.SMEM)
HBM = pl.BlockSpec(memory_space=pltpu.HBM)
ANY = pl.BlockSpec(memory_space=pl.ANY)
F32 = jnp.float32
LIGHT = pl.CostEstimate(flops=1, bytes_accessed=1, transcendentals=0)


def pairs(move):
    found = []
    for index in range(32):
        y, x, z, core = index // 16, index // 8 % 2, index // 2 % 4, index % 2
        y, x, z, core = move(y, x, z, core)
        found.append((index, y * 16 + x * 8 + z * 2 + core))
    return found


PLANE_FIRST = pairs(lambda y, x, z, c: (y, 1 - x, z, c) if c == 0 else (1 - y, x, z, c))
PLANE_SECOND = pairs(lambda y, x, z, c: (1 - y, x, z, c) if c == 0 else (y, 1 - x, z, c))
CORES = pairs(lambda y, x, z, c: (y, x, z, 1 - c))
LINE_FIRST = pairs(lambda y, x, z, c: (y, x, z ^ (1 if c == 0 else 2), c))
LINE_SECOND = pairs(lambda y, x, z, c: (y, x, z ^ (2 if c == 0 else 1), c))


def loads_kernel(first, place, probes, dosage, mean, *refs):
    count = len(CHUNKS)
    if first:
        parts, (probe_b, sums, held, wide, middles, sem, sem_p, sem_m) = refs[:count], refs[count:]
    else:
        sums_in, parts, (held, sem) = refs[0], refs[2 : 2 + count], refs[2 + count :]
    slot = 0 if first else 1
    _, rows, width = held.shape
    block = rows // STEPS
    half = 1 - place[0] if first else place[0]
    start = pl.multiple_of(half * width, width)

    def copies(step):
        at = pl.ds(step * block, block)
        made = [pltpu.make_async_copy(dosage.at[at, pl.ds(start, width)], held.at[slot, at], sem.at[step])]
        if first:
            made.append(pltpu.make_async_copy(probes.at[:, at], wide.at[:, at], sem_p.at[step]))
        return made

    for step in range(STEPS):
        for copy in copies(step):
            copy.start()
    if first:
        copy_mean = pltpu.make_async_copy(mean, middles, sem_m)
        copy_mean.start()
    for step in range(STEPS):
        at = pl.ds(step * block, block)
        for copy in copies(step):
            copy.wait()
        if first:
            left = wide[:, at].astype(jnp.bfloat16)
            probe_b[:, at] = left
            share = jnp.sum(left.astype(F32), axis=1, keepdims=True)
            total = share if step == 0 else total + share
        else:
            left = probes[:, at]
        right = held[slot, at]
        product = jnp.dot(left, right, preferred_element_type=F32)
        low = 0
        for part, many in zip(parts, CHUNKS):
            if step == 0:
                part[...] = product[low : low + many]
            else:
                part[...] += product[low : low + many]
            low += many
    if first:
        sums[...] = jnp.broadcast_to(total, sums.shape)
        copy_mean.wait()
        middle = middles[:, pl.ds(start, width)]
    else:
        total = sums_in[:, :1]
        middle = mean[:, pl.ds(start, width)]
    low = 0
    for part, many in zip(parts, CHUNKS):
        part[...] -= total[low : low + many] * middle
        low += many


def in_hbm(*arrays):
    return [pltpu.with_memory_space_constraint(array, pltpu.HBM) for array in arrays]


def in_vmem(*arrays):
    return [pltpu.with_memory_space_constraint(array, pltpu.VMEM) for array in arrays]


def first_half(place, probes, dosage, mean):
    count, rows = probes.shape
    width = dosage.shape[1] // 2
    return pl.pallas_call(
        functools.partial(loads_kernel, True),
        in_specs=[SMEM, HBM, HBM, HBM],
        out_specs=[VMEM] * (len(CHUNKS) + 3),
        out_shape=[jax.ShapeDtypeStruct((many, width), F32) for many in CHUNKS]
        + [
            jax.ShapeDtypeStruct((count, rows), jnp.bfloat16),
            jax.ShapeDtypeStruct((count, 128), F32),
            pltpu.VMEM((2, rows, width), jnp.bfloat16),
        ],
        scratch_shapes=[
            pltpu.VMEM((count, rows), F32),
            pltpu.VMEM((1, 2 * width), F32),
            pltpu.SemaphoreType.DMA((STEPS,)),
            pltpu.SemaphoreType.DMA((STEPS,)),
            pltpu.SemaphoreType.DMA,
        ],
        compiler_params=pltpu.CompilerParams(vmem_limit_bytes=LIMIT),
        cost_estimate=LIGHT,
        name="loads_sent",
    )(place, *in_hbm(probes, dosage, mean))


def second_half(place, probe_b, dosage, mean, sums, held):
    count, rows = probe_b.shape
    width = dosage.shape[1] // 2
    return pl.pallas_call(
        functools.partial(loads_kernel, False),
        in_specs=[SMEM, VMEM, HBM] + [VMEM] * 3,
        out_specs=[VMEM] * (len(CHUNKS) + 1),
        out_shape=[jax.ShapeDtypeStruct((many, width), F32) for many in CHUNKS]
        + [pltpu.VMEM((2, rows, width), jnp.bfloat16)],
        scratch_shapes=[pltpu.SemaphoreType.DMA((STEPS,))],
        input_output_aliases={5: len(CHUNKS)},
        compiler_params=pltpu.CompilerParams(vmem_limit_bytes=LIMIT),
        cost_estimate=LIGHT,
        name="loads_kept",
    )(place, probe_b, *in_hbm(dosage), mean, sums, *in_vmem(held))


def add_kernel(count, order, *refs):
    values, outs = refs[:count], refs[count + order :]
    width = outs[0].shape[1]
    whole, pieces = values[0], values[1:]
    if pieces[0].shape[1] < whole.shape[1]:
        narrow = pieces[0].shape[1]
        for index, piece in enumerate(pieces):
            low = index * narrow
            outs[low // width][:, low % width : low % width + narrow] = whole[:, low : low + narrow] + piece[...]
        return
    total = whole[...]
    for value in pieces:
        total = total + value[...]
    for index, out in enumerate(outs):
        out[...] = total[:, index * width : (index + 1) * width]


def add_up(*arrays, after=(), cut=1):
    many, width = arrays[0].shape
    count = len(arrays)
    return pl.pallas_call(
        functools.partial(add_kernel, count, len(after)),
        in_specs=[VMEM] * count + [ANY] * len(after),
        out_specs=[VMEM] * cut,
        out_shape=[jax.ShapeDtypeStruct((many, width // cut), F32)] * cut,
        compiler_params=pltpu.CompilerParams(vmem_limit_bytes=LIMIT),
        cost_estimate=LIGHT,
        name="add_up",
    )(*arrays, *after)


def halves_kernel(count, *refs):
    whole, received, (out, *halves) = refs[0], refs[1 : 1 + count], refs[-3:]
    width = halves[0].shape[1]
    for index, half in enumerate(halves):
        at = slice(index * width, (index + 1) * width)
        value = whole[:, at] + (received[0][:, at] if count == 1 else received[index][...])
        out[:, at] = value
        half[...] = value


def add_halves(whole, received, after=()):
    many, width = whole.shape
    return pl.pallas_call(
        functools.partial(halves_kernel, len(received)),
        in_specs=[VMEM] * (1 + len(received)) + [ANY] * len(after),
        out_specs=[VMEM] * 3,
        out_shape=[jax.ShapeDtypeStruct((many, wide), F32) for wide in (width, width // 2, width // 2)],
        compiler_params=pltpu.CompilerParams(vmem_limit_bytes=LIMIT),
        cost_estimate=LIGHT,
        name="add_halves",
    )(whole, *received, *after)


def scaled(loads, gain, middle, factor):
    left = (loads * (gain * gain * factor)).astype(jnp.bfloat16)
    return left, jnp.sum(left.astype(F32) * middle, axis=1, keepdims=True)


def blocks(place, held, swapped):
    core, z = place[1], place[2]
    block = held.shape[1] // 8
    mask = 2 - core if swapped else 1 + core
    flips = [(3 - mask, 1 - core), (3, 1 - core), (mask, core), (3, core)]
    flips += [(0, 1 - core), (mask, 1 - core), (0, core), (3 - mask, core)]
    return [pl.ds(pl.multiple_of(((z ^ flip) * 2 + owner) * block, block), block) for flip, owner in flips]


def times(left, held, slot, at):
    return lax.dot_general(left, held[slot, at], (((1,), (1,)), ((), ())), preferred_element_type=F32)


def half_span(half, width):
    return pl.ds(pl.multiple_of(half * width, width), width)


def own_kernel(swapped, factor, place, own, mean, scale, held, *refs):
    partial, shift_out = refs[-2:]
    span = half_span(place[0], own.shape[1])
    left, shift = scaled(own[...], scale[:, span], mean[:, span], factor)
    shift_out[...] = jnp.broadcast_to(shift, shift_out.shape)
    block = held.shape[1] // 8
    for index, at in enumerate(blocks(place, held, swapped)):
        partial[:, index * block : (index + 1) * block] = times(left, held, 1, at)


def apply_kernel(first, split, swapped, factor, shrink, place, *refs):
    if first:
        other, own, mean, scale, held = refs[:5]
        *pieces, kept, left_out, shift_out = refs[-3 - PIECES :]
        other = other[...]
        if split:
            other = jnp.concatenate([other, refs[6][...]], axis=1)
        span = half_span(1 - place[0], other.shape[1])
        left, shift = scaled(other, scale[:, span], mean[:, span], factor)
        left_out[0] = left
        lefts = [left]
        if split:
            partial, shift_own = own, refs[5][:, :1]
        else:
            span = half_span(place[0], own.shape[1])
            left, shift_own = scaled(own[...], scale[:, span], mean[:, span], factor)
            left_out[1] = left
            lefts.append(left)
        shift = (shift + shift_own) * shrink
        shift_out[...] = jnp.broadcast_to(shift, shift_out.shape)
    else:
        left_in, shift_in, held = refs[:3]
        *pieces, kept = refs[-1 - PIECES :]
        lefts = [left_in[slot] for slot in range(left_in.shape[0])]
        shift = shift_in[:, :1]
        if split:
            partial = refs[3]
    block = held.shape[1] // 8
    skip = 0 if first else 4
    spans = blocks(place, held, swapped)[skip : skip + 4]
    for index, at in enumerate(spans):
        product = 0.0
        if split:
            low = (skip + index) * block
            product = partial[:, low : low + block]
        for slot, left in enumerate(lefts):
            product = product + times(left, held, slot, at)
        product = product * shrink - shift
        outs, start = (pieces, index * block) if index < 2 else ([kept], (index - 2) * block)
        width = outs[0].shape[1]
        step = min(width, block)
        for part in range(0, block, step):
            place_in = start + part
            outs[place_in // width][:, place_in % width : place_in % width + step] = product[:, part : part + step]


def own_rows(factor, place, own, mean, scale, held, after, swapped=False):
    many = own.shape[0]
    return pl.pallas_call(
        functools.partial(own_kernel, swapped, factor),
        in_specs=[SMEM] + [VMEM] * 4 + [ANY] * len(after),
        out_specs=[VMEM] * 2,
        out_shape=[jax.ShapeDtypeStruct((many, held.shape[1]), F32), jax.ShapeDtypeStruct((many, 128), F32)],
        compiler_params=pltpu.CompilerParams(vmem_limit_bytes=LIMIT),
        cost_estimate=LIGHT,
        name="own_rows",
    )(place, own, mean, scale, *in_vmem(held), *after)


def apply_rows(first, factor, shrink, place, *arrays, held, after, split=False, swapped=False):
    many = arrays[0].shape[-2]
    place_of_held = 4 if first else 2
    wide = held.shape[1] // 4
    out_shape = [jax.ShapeDtypeStruct((many, wide // PIECES), F32)] * PIECES
    out_shape += [jax.ShapeDtypeStruct((many, wide), F32)]
    if first:
        out_shape += [
            jax.ShapeDtypeStruct((1 if split else 2, many, held.shape[2]), jnp.bfloat16),
            jax.ShapeDtypeStruct((many, 128), F32),
        ]
    return pl.pallas_call(
        functools.partial(apply_kernel, first, split, swapped, factor, shrink),
        in_specs=[SMEM] + [VMEM] * (len(arrays) + 1) + [ANY] * len(after),
        out_specs=[VMEM] * len(out_shape),
        out_shape=out_shape,
        compiler_params=pltpu.CompilerParams(vmem_limit_bytes=LIMIT),
        cost_estimate=LIGHT,
        name="apply_first" if first else "apply_second",
    )(place, *arrays[:place_of_held], *in_vmem(held), *arrays[place_of_held:], *after)


def on_slice(dosage, allele_mean, allele_scale, probes):
    total = dosage.shape[0] * lax.axis_size("sample")
    across = dosage.shape[1] * lax.axis_size("snp")
    sample, snp = lax.axis_index("sample"), lax.axis_index("snp")
    core, z = snp % 2, snp // 2
    half = jnp.where(core == 0, sample % 2, sample // 2)
    place = jnp.stack([half, core, z]).astype(jnp.int32)
    mean, scale = allele_mean[None, :], allele_scale[None, :]
    factor, shrink = total**-0.5, across**-0.5
    send = lambda array, moves: lax.ppermute(array, AXES, moves)

    apply_first = functools.partial(apply_rows, True, factor, shrink, place)
    apply_second = functools.partial(apply_rows, False, factor, shrink, place)

    sent_a, sent_b, probe_b, sums, held = first_half(place, probes, dosage, mean)
    got_a, got_b = send(sent_a, PLANE_FIRST), send(sent_b, PLANE_FIRST)
    own_a, own_b, held = second_half(place, probe_b, dosage, mean, sums, held)
    own_a, *parts = add_halves(own_a, [got_a])
    got_a = [send(part, PLANE_SECOND) for part in parts]
    (own_b,) = add_up(own_b, got_b, after=[own_a])
    got_b = send(own_b, PLANE_SECOND)
    own_a, *parts = add_halves(own_a, got_a, after=[own_b])
    other_a = [send(part, PLANE_FIRST) for part in parts]
    part_a, shift_a = own_rows(factor, place, own_a, mean, scale, held, after=[])
    (own_b,) = add_up(own_b, got_b, after=[part_a])
    other_b = send(own_b, PLANE_FIRST)
    *sent, far_a, left_a, shift_a = apply_first(
        other_a[0], part_a, mean, scale, shift_a, other_a[1], held=held, after=[own_b], split=True
    )
    (far_a,) = add_up(far_a, *[send(piece, CORES) for piece in sent])
    got_a = send(far_a, LINE_FIRST)
    *sent, near_a = apply_second(left_a, shift_a, part_a, held=held, after=[far_a], split=True)
    core_a = [send(piece, CORES) for piece in sent]
    *sent, far_b, left_b, shift_b = apply_first(
        other_b, own_b, mean, scale, held=held, after=[near_a], swapped=True
    )
    (far_b,) = add_up(far_b, *[send(piece, CORES) for piece in sent])
    got_b = send(far_b, LINE_SECOND)
    (near_a,) = add_up(near_a, got_a, after=[far_b])
    near_a, sent_a = add_up(near_a, *core_a, cut=2)
    got_a = send(sent_a, LINE_SECOND)
    *sent, near_b = apply_second(left_b, shift_b, held=held, after=[near_a], swapped=True)
    core_b = [send(piece, CORES) for piece in sent]
    (near_b,) = add_up(near_b, got_b, after=[near_a])
    near_b, sent_b = add_up(near_b, *core_b, cut=2)
    got_b = send(sent_b, LINE_FIRST)
    return jnp.concatenate([near_a + got_a, near_b + got_b], axis=0)


def on_any(dosage, allele_mean, allele_scale, probes):
    rows = dosage.shape[0]
    total = rows * lax.axis_size("sample")
    width = dosage.shape[1] * lax.axis_size("snp")
    genos = ((dosage.astype(jnp.float32) - allele_mean[None, :]) * allele_scale[None, :]).astype(
        jnp.bfloat16
    )
    probe_b = probes.astype(jnp.bfloat16)
    local = jnp.dot(probe_b, genos, preferred_element_type=jnp.float32)
    loads = lax.psum(local, "sample")
    loads_b = (loads / jnp.sqrt(jnp.float32(total))).astype(jnp.bfloat16)
    partial_rows = lax.dot_general(
        loads_b, genos, (((1,), (1,)), ((), ())), preferred_element_type=jnp.float32
    )
    summed = lax.psum_scatter(partial_rows, "snp", scatter_dimension=1, tiled=True)
    return summed / jnp.sqrt(jnp.float32(width))


def solution(mesh):
    placed = (P("sample", "snp"), P("snp"), P("snp"), P(None, "sample"))
    body = on_slice if (mesh.shape["sample"], mesh.shape["snp"]) == (4, 8) else on_any
    return jax.shard_map(
        body, mesh=mesh, in_specs=placed, out_specs=P(None, ("sample", "snp")), check_vma=False
    )
```
